32 devices in a mesh: seq: 8 (over z, x), head: 4 (over y, core).
Axes of the slice: x: 2, y: 2, z: 4, core: 2. Of those that a mesh axis runs over, the one named last changes fastest.
Arguments:
- x_inputs: bfloat16 [65536, 1024], P('seq', 'head'), may hold values from -6 to 6
- x_in_proj: bfloat16 [65536, 128], P('seq'), may hold values from -0.5 to 0.5
- x_out_proj: bfloat16 [65536, 128], P('seq'), may hold values from -6 to 6
- x_log_decay: float32 [16, 65536], P('head', 'seq'), may hold values from -0.6 to 0
- x_step: float32 [16, 65536], P('head', 'seq'), may hold values from 0 to 0.5
- z_source: int32 [65536], P('seq'), may hold values from 0 to 65535, as said below
- z_in_proj: bfloat16 [65536, 128], P('seq'), may hold values from -0.5 to 0.5
- z_out_proj: bfloat16 [65536, 128], P('seq'), may hold values from -6 to 6
- z_log_decay: float32 [16, 65536], P('head', 'seq'), may hold values from -0.6 to 0
- z_step: float32 [16, 65536], P('head', 'seq'), may hold values from 0 to 0.5
- gate_branch: bfloat16 [65536, 1024], P('seq', 'head'), may hold values from -8 to 8
- norm_gain: float32 [1024], P('head'), may hold values from 0.1 to 1.9
- out_weight: bfloat16 [1024, 512], P('head'), may hold values from -0.1875 to 0.1875
Outputs:
- layer_out: bfloat16 [65536, 512], P(('seq', 'head'))
The draws below stay inside these ranges and needn't reach their ends.
Inputs may be any that keep to these rules, and one draw needn't show every extreme that they name: z_source is a permutation; every block of 8192 consecutive z-order positions takes exactly 1024 tokens from each block of 8192 consecutive x-order tokens.
All inputs are finite; a program needn't handle non-finite values.
Results may differ from the reference program's by a relative error of at most 0.034.
Values may be sent and summed in bfloat16 or wider, within the bound.
A program may use at most 128 MiB of HBM per device.

```python
import math
import jax
import jax.numpy as jnp
from jax import lax

D = 512
HEADS = 16
HEAD_DIM = 64
STATE = 128
BLOCK = 512
TOK_DEV = 8192
HP = 1024
TOKENS = 65536
PEER_ROWS = 1024
N_HEAD = 4


def head_rate(key, salt):
    order = jax.random.permutation(jax.random.fold_in(key, salt), HEADS).astype(jnp.float32)
    offset = jax.random.uniform(jax.random.fold_in(key, salt + 5), (HEADS,))
    low = math.log(1.0 / (8.0 * BLOCK))
    high = math.log(1.0 / 32.0)
    return jnp.exp(low + (high - low) * (order + offset) / HEADS)


def decay_draw(key, salt):
    decay_speed = head_rate(key, salt)[:, None]
    spread = math.log(2.0)
    coarse_estimate = jnp.exp(jax.random.uniform(jax.random.fold_in(key, salt + 1), (HEADS, TOKENS), jnp.float32, -spread, spread))
    patch_locations = jax.random.randint(jax.random.fold_in(key, salt + 2), (HEADS, 2), 0, TOKENS)
    token_place = jnp.arange(TOKENS, dtype=jnp.int32)[None, :]
    sudden_spike = (token_place == patch_locations[:, 0:1]) | (token_place == patch_locations[:, 1:2])
    retained_mask = jax.random.uniform(jax.random.fold_in(key, salt + 3), (HEADS, TOKENS), jnp.float32, 0.6, 0.8)
    return -decay_speed * coarse_estimate + jnp.where(sudden_spike, jnp.log(retained_mask), 0.0)


def step_draw(key, salt):
    decay_speed = head_rate(key, salt)[:, None]
    spread = math.log(2.0)
    coarse_estimate = jnp.exp(jax.random.uniform(jax.random.fold_in(key, salt + 4), (HEADS, TOKENS), jnp.float32, -spread, spread))
    return jnp.sqrt(2.0 * decay_speed) * coarse_estimate


def draw_x_log_decay(key, part):
    return decay_draw(key, 11)


def draw_x_step(key, part):
    return step_draw(key, 11)


def draw_z_log_decay(key, part):
    return decay_draw(key, 31)


def draw_z_step(key, part):
    return step_draw(key, 31)


def draw_z_source(key, part):
    group_sets = TOK_DEV // PEER_ROWS
    keys_dest = jax.random.split(jax.random.fold_in(key, 51), group_sets)
    keys_source = jax.random.split(jax.random.fold_in(key, 52), group_sets)
    sigma = jax.vmap(lambda subkey: jax.random.permutation(subkey, TOK_DEV))(keys_dest)
    tau = jax.vmap(lambda subkey: jax.random.permutation(subkey, TOK_DEV))(keys_source)
    source = sigma % group_sets
    slot = jnp.arange(group_sets, dtype=jnp.int32)[:, None] * PEER_ROWS + sigma // group_sets
    result = source * TOK_DEV + tau[source, slot]
    return result.reshape(TOKENS).astype(jnp.int32)


def draw_gate_branch(key, part):
    channel = jnp.arange(HP, dtype=jnp.float32) / HP
    noise = jnp.clip(jax.random.normal(jax.random.fold_in(key, 71), (TOKENS, HP), jnp.float32), -4.0, 4.0)
    scale = 0.6 * jnp.power(3.0, channel)
    return (noise * scale[None, :]).astype(jnp.bfloat16)


def levels(own_key, shape, cuts, low, top_value):
    factor_of, own = 1.0, jax.random.fold_in(own_key, 6)
    for axis_at, shards_of in cuts:
        steps = jnp.exp(jax.random.uniform(jax.random.fold_in(own, axis_at), (shards_of,), jnp.float32, low / len(cuts), top_value / len(cuts)))
        factor_of = factor_of * jnp.repeat(steps, shape[axis_at] // shards_of).reshape([-1 if axis == axis_at else 1 for axis in range(len(shape))])
    return factor_of


def normal_values(own_key, shape, deviation, most, cuts=(), kind=jnp.bfloat16):
    entries = deviation * jax.random.normal(own_key, shape, jnp.float32)
    if cuts:
        entries = entries * levels(own_key, shape, cuts, -0.22, 0.18)
    return jnp.clip(entries, -most, most).astype(kind)


def setup_inputs(seed: int = 0) -> dict:
    arg_keys = jax.random.split(jax.random.key(seed), 14)
    x_inputs = normal_values(arg_keys[0], (TOKENS, HP), 1.0, 6.0, ((0, 8), (1, 4)))
    x_in_proj = normal_values(arg_keys[1], (TOKENS, STATE), STATE ** -0.5, 0.5, ((0, 8),))
    x_out_proj = normal_values(arg_keys[2], (TOKENS, STATE), 1.0, 6.0, ((0, 8),))
    x_log_decay = draw_x_log_decay(jax.random.fold_in(arg_keys[13], 71), 0)
    x_step = draw_x_step(jax.random.fold_in(arg_keys[13], 71), 0)
    z_source = draw_z_source(jax.random.fold_in(arg_keys[13], 71), 0)
    z_in_proj = normal_values(arg_keys[6], (TOKENS, STATE), STATE ** -0.5, 0.5, ((0, 8),))
    z_out_proj = normal_values(arg_keys[7], (TOKENS, STATE), 1.0, 6.0, ((0, 8),))
    z_log_decay = draw_z_log_decay(jax.random.fold_in(arg_keys[13], 71), 0)
    z_step = draw_z_step(jax.random.fold_in(arg_keys[13], 71), 0)
    gate_branch = draw_gate_branch(jax.random.fold_in(arg_keys[13], 71), 0)
    norm_gain = jnp.clip(1.0 + 0.18 * jax.random.normal(arg_keys[11], (HP,), jnp.float32), 0.1, 1.9)
    out_weight = normal_values(arg_keys[12], (HP, D), HP ** -0.5, 0.1875, ((0, 4),))
    return {"x_inputs": x_inputs, "x_in_proj": x_in_proj, "x_out_proj": x_out_proj, "x_log_decay": x_log_decay, "x_step": x_step, "z_source": z_source, "z_in_proj": z_in_proj, "z_out_proj": z_out_proj, "z_log_decay": z_log_decay, "z_step": z_step, "gate_branch": gate_branch, "norm_gain": norm_gain, "out_weight": out_weight}


def round_half(value):
    return lax.optimization_barrier(value.astype(jnp.bfloat16)).astype(jnp.float32)

def ssd_scan(inputs, b_mat, c_mat, log_decay, step):
    count = inputs.shape[0]
    blocks = count // BLOCK
    u_blocks = inputs.reshape(blocks, BLOCK, HEADS, HEAD_DIM)
    b_blocks = b_mat.reshape(blocks, BLOCK, STATE)
    c_blocks = c_mat.reshape(blocks, BLOCK, STATE)
    g_blocks = log_decay.reshape(HEADS, blocks, BLOCK).transpose(1, 0, 2)
    d_blocks = step.reshape(HEADS, blocks, BLOCK).transpose(1, 0, 2)
    rows = lax.broadcasted_iota(jnp.int32, (BLOCK, BLOCK), 0)
    cols = lax.broadcasted_iota(jnp.int32, (BLOCK, BLOCK), 1)
    lower = rows >= cols

    def one_block(carry, pieces):
        u_blk, b_blk, c_blk, g_blk, d_blk = pieces
        cum = jnp.cumsum(g_blk, axis=1)
        tot = cum[:, -1]
        scores = jnp.dot(c_blk, b_blk.T, preferred_element_type=jnp.float32)
        diff = jnp.where(lower[None], cum[:, :, None] - cum[:, None, :], -jnp.inf)
        weights = round_half(scores[None] * jnp.exp(diff) * d_blk[:, None, :])
        u_float = u_blk.astype(jnp.float32)
        intra = jnp.einsum('hts,shp->thp', weights, u_float)
        scale = (jnp.exp(tot[:, None] - cum) * d_blk).T
        contrib = round_half(u_float * scale[:, :, None])
        state_add = jnp.einsum('shp,sn->hpn', contrib, b_blk.astype(jnp.float32))
        inter = jnp.einsum('tn,hpn->thp', c_blk.astype(jnp.float32), round_half(carry))
        inter = inter * jnp.exp(cum).T[:, :, None]
        result = (intra + inter).astype(jnp.bfloat16).reshape(BLOCK, HEADS * HEAD_DIM)
        carry = jnp.exp(tot)[:, None, None] * carry + state_add
        return (carry, result)
    start = jnp.zeros((HEADS, HEAD_DIM, STATE), jnp.float32)
    _, outputs = lax.scan(one_block, start, (u_blocks, b_blocks, c_blocks, g_blocks, d_blocks))
    return outputs.reshape(count, HEADS * HEAD_DIM)

def reference(x_inputs, x_in_proj, x_out_proj, x_log_decay, x_step, z_source, z_in_proj, z_out_proj, z_log_decay, z_step, gate_branch, norm_gain, out_weight):
    y_x = ssd_scan(x_inputs, x_in_proj, x_out_proj, x_log_decay, x_step)
    u_z = jnp.take(y_x, z_source.astype(jnp.int32), axis=0)
    y_z = ssd_scan(u_z, z_in_proj, z_out_proj, z_log_decay, z_step)
    gated = y_z.astype(jnp.float32) * jax.nn.silu(gate_branch.astype(jnp.float32))
    mean_square = lax.optimization_barrier(jnp.mean(gated * gated, axis=1, keepdims=True))
    normed = (gated * lax.rsqrt(mean_square + 1e-05) * norm_gain).astype(jnp.bfloat16)
    group = HP // N_HEAD
    total = jnp.zeros((normed.shape[0], D), jnp.float32)
    for index in range(N_HEAD):
        partial_sum = jnp.dot(normed[:, index * group:(index + 1) * group], out_weight[index * group:(index + 1) * group], preferred_element_type=jnp.float32)
        total = total + round_half(partial_sum)
    return total.astype(jnp.bfloat16)
```

```python
import functools
import math

import jax
import jax.numpy as jnp
from jax import lax
from jax.experimental import pallas as pl
from jax.experimental.pallas import tpu as pltpu
from jax.sharding import PartitionSpec as P

CHUNK = 256
STEP = 1024
UNROLL = 32
VMEM = 56 * 1024 * 1024
LOG2E = math.log2(math.e)


def spread(columns, first, heads, width):
    head_width = width // heads
    rows = columns.shape[0]
    lanes = lax.broadcasted_iota(jnp.int32, (rows, width), 1)
    out = jnp.broadcast_to(columns[:, first : first + 1], (rows, width))
    for h in range(1, heads):
        column = jnp.broadcast_to(columns[:, first + h : first + h + 1], (rows, width))
        out = jnp.where(lanes >= h * head_width, column, out)
    return out


def add_state(total, u, b, columns, heads):
    width = u.shape[1]
    scale = spread(columns, 3 * heads, heads, width)
    contrib = (u.astype(jnp.float32) * scale).astype(jnp.bfloat16)
    total[...] += lax.dot_general(
        b, contrib, (((0,), (0,)), ((), ())), preferred_element_type=jnp.float32
    )


def final_kernel(heads, u_ref, b_ref, col_ref, out_ref, total):
    @pl.when(pl.program_id(0) == 0)
    def _():
        total[...] = jnp.zeros_like(total)

    add_state(total, u_ref[...], b_ref[...], col_ref[...], heads)
    out_ref[...] = total[...].astype(out_ref.dtype)


def place_kernel(heads, place_ref, recv_ref, b_ref, col_ref, out_ref, u_out, total, held, stage):
    step = pl.program_id(0)

    @pl.when(step == 0)
    def _():
        total[...] = jnp.zeros_like(total)

        def rows(i, _):
            base = pl.multiple_of(i * UNROLL, UNROLL)
            stage[...] = recv_ref[pl.ds(base, UNROLL), :].astype(jnp.float32)
            for r in range(UNROLL):
                held[pl.ds(place_ref[base + r], 1), :] = stage[r : r + 1, :]
            return 0

        lax.fori_loop(0, recv_ref.shape[0] // UNROLL, rows, 0)

    count = b_ref.shape[0]
    u = held[pl.ds(pl.multiple_of(step * count, count), count), :].astype(jnp.bfloat16)
    u_out[...] = u
    add_state(total, u, b_ref[...], col_ref[...], heads)
    out_ref[...] = total[...].astype(out_ref.dtype)


def chunk_result(heads, u, b, c, columns, rows, state):
    count, width = u.shape
    head_width = width // heads
    scores = lax.dot_general(c, b, (((1,), (1,)), ((), ())), preferred_element_type=jnp.float32)
    lower = lax.broadcasted_iota(jnp.int32, (count, count), 0) >= lax.broadcasted_iota(
        jnp.int32, (count, count), 1
    )
    lanes = lax.broadcasted_iota(jnp.int32, (count, width), 1)
    grow = spread(columns, 2 * heads, heads, width)
    y = grow * jnp.dot(c, state[...].astype(jnp.bfloat16), preferred_element_type=jnp.float32)
    weights, inputs = [], []
    for h in range(heads):
        factor = jnp.exp2(columns[:, h : h + 1] - rows[h : h + 1, :])
        weights.append(jnp.where(lower, scores * factor, 0.0).astype(jnp.bfloat16))
        mine = (lanes >= h * head_width) & (lanes < (h + 1) * head_width)
        inputs.append(jnp.where(mine, u, jnp.zeros_like(u)))
    y += jnp.dot(
        jnp.concatenate(weights, axis=1),
        jnp.concatenate(inputs, axis=0),
        preferred_element_type=jnp.float32,
    )
    scale = spread(columns, heads, heads, width)
    contrib = (u.astype(jnp.float32) * scale).astype(jnp.bfloat16)
    state[...] = grow[count - 1 : count, :] * state[...] + lax.dot_general(
        b, contrib, (((0,), (0,)), ((), ())), preferred_element_type=jnp.float32
    )
    return y


def scan_gather_kernel(
    heads, pick_ref, u_ref, b_ref, c_ref, col_ref, row_ref, start_ref, out_ref, state, held, stage
):
    step = pl.program_id(0)

    @pl.when(step == 0)
    def _():
        state[...] = start_ref[...]

    y = chunk_result(
        heads, u_ref[...], b_ref[...], c_ref[...], col_ref[...], row_ref[0], state
    )
    held[pl.ds(pl.multiple_of(step * CHUNK, CHUNK), CHUNK), :] = y

    @pl.when(step == pl.num_programs(0) - 1)
    def _():
        def rows(i, _):
            base = pl.multiple_of(i * UNROLL, UNROLL)
            for r in range(UNROLL):
                stage[r : r + 1, :] = held[pl.ds(pick_ref[base + r], 1), :]
            out_ref[pl.ds(base, UNROLL), :] = stage[...].astype(out_ref.dtype)
            return 0

        lax.fori_loop(0, out_ref.shape[0] // UNROLL, rows, 0)


def scan_gate_kernel(
    heads, u_ref, b_ref, c_ref, col_ref, row_ref, start_ref, gate_ref, out_ref, state
):
    @pl.when(pl.program_id(0) == 0)
    def _():
        state[...] = start_ref[...]

    y = chunk_result(
        heads, u_ref[...], b_ref[...], c_ref[...], col_ref[...], row_ref[0], state
    )
    gate = gate_ref[...].astype(jnp.float32)
    out_ref[...] = (y * gate / (1.0 + jnp.exp(-gate))).astype(out_ref.dtype)


def tail_kernel(g_ref, gain_ref, w_ref, out_ref):
    groups, rows, width = g_ref.shape
    square = jnp.zeros((rows, 1), jnp.float32)
    for k in range(groups):
        g = g_ref[k].astype(jnp.float32)
        square += jnp.sum(g * g, axis=1, keepdims=True)
    inverse = lax.rsqrt(square / (groups * width) + 1e-05)
    total = jnp.zeros(out_ref.shape, jnp.float32)
    for k in range(groups):
        normed = (g_ref[k].astype(jnp.float32) * inverse * gain_ref[k : k + 1, :]).astype(
            jnp.bfloat16
        )
        total += jnp.dot(normed, w_ref[k], preferred_element_type=jnp.float32)
    out_ref[...] = total.astype(out_ref.dtype)


def params():
    return pltpu.CompilerParams(vmem_limit_bytes=VMEM)


def by_row(rows, width):
    return pl.BlockSpec((rows, width), lambda i: (i, 0))


def whole(*shape):
    return pl.BlockSpec(shape, lambda i: (0,) * len(shape))


def smem():
    return pl.BlockSpec(memory_space=pltpu.SMEM)


def f32(*shape):
    return pltpu.VMEM(shape, jnp.float32)


def bf16(*shape):
    return jax.ShapeDtypeStruct(shape, jnp.bfloat16)


def decay_tables(log_decay, step):
    heads, count = log_decay.shape
    chunks = count // CHUNK
    ones = jnp.triu(jnp.ones((CHUNK, CHUNK), jnp.float32))
    g = log_decay.reshape(heads * chunks, CHUNK) * LOG2E
    cum = jnp.dot(g, ones, precision=lax.Precision.HIGHEST).reshape(heads, chunks, CHUNK)
    dt = step.reshape(heads, chunks, CHUNK)
    totals = cum[:, :, -1]
    after = lax.cumsum(totals, axis=1, reverse=True) - totals
    rest = totals[:, :, None] - cum
    columns = jnp.concatenate(
        [cum, jnp.exp2(rest) * dt, jnp.exp2(cum), jnp.exp2(rest + after[:, :, None]) * dt]
    )
    rows = (cum - jnp.log2(dt)).transpose(1, 0, 2)
    return columns.reshape(4 * heads, count).T, rows, jnp.sum(totals, axis=1)


def start_state(final, totals, width):
    me = lax.axis_index("seq")
    finals = lax.all_gather(final, "seq")
    count, heads = totals.shape
    place = jnp.arange(count)
    between = (place[None, :] > place[:, None]) & (place[None, :] < me)
    log = jnp.sum(jnp.where(between[:, :, None], totals[None], 0.0), axis=1)
    coef = jnp.where(place[:, None] < me, jnp.exp2(log), 0.0)
    coef = jnp.repeat(coef, width // heads, axis=1)
    return jnp.sum(coef[:, None, :] * finals.astype(jnp.float32), axis=0)


def body(
    x_inputs,
    x_in_proj,
    x_out_proj,
    x_log_decay,
    x_step,
    z_source,
    z_in_proj,
    z_out_proj,
    z_log_decay,
    z_step,
    gate_branch,
    norm_gain,
    out_weight,
):
    count, width = x_inputs.shape
    heads = x_log_decay.shape[0]
    state = x_in_proj.shape[1]
    peers = lax.axis_size("seq")
    groups = lax.axis_size("head")
    share = count // peers
    big = min(STEP, count)

    order, place = lax.sort((z_source, lax.iota(jnp.int32, count)), num_keys=1)
    pick = order.reshape(peers, share) - lax.iota(jnp.int32, peers)[:, None] * count
    pick = lax.all_to_all(pick, "seq", 0, 0).reshape(count)

    x_cols, x_rows, x_total = decay_tables(x_log_decay, x_step)
    z_cols, z_rows, z_total = decay_tables(z_log_decay, z_step)
    totals = lax.all_gather(jnp.stack([x_total, z_total]), "seq")
    weight = lax.all_gather(out_weight, "head")
    gain = lax.all_gather(norm_gain, "head")

    cols = x_cols.shape[1]
    chunk_specs = [
        by_row(CHUNK, width),
        by_row(CHUNK, state),
        by_row(CHUNK, state),
        by_row(CHUNK, cols),
        pl.BlockSpec((1, heads, CHUNK), lambda i: (i, 0, 0)),
        whole(state, width),
    ]

    x_final = pl.pallas_call(
        functools.partial(final_kernel, heads),
        out_shape=bf16(state, width),
        grid=(count // big,),
        in_specs=[by_row(big, width), by_row(big, state), by_row(big, cols)],
        out_specs=whole(state, width),
        scratch_shapes=[f32(state, width)],
        compiler_params=params(),
        name="x_final",
    )(x_inputs, x_in_proj, x_cols)
    x_start = start_state(x_final, totals[:, 0], width)
    sent = pl.pallas_call(
        functools.partial(scan_gather_kernel, heads),
        out_shape=bf16(count, width),
        grid=(count // CHUNK,),
        in_specs=[smem()] + chunk_specs,
        out_specs=whole(count, width),
        scratch_shapes=[f32(state, width), f32(count, width), f32(UNROLL, width)],
        compiler_params=params(),
        name="x_scan",
    )(pick, x_inputs, x_in_proj, x_out_proj, x_cols, x_rows, x_start)

    received = lax.all_to_all(sent.reshape(peers, share, width), "seq", 0, 0)
    received = received.reshape(count, width)

    z_final, u_z = pl.pallas_call(
        functools.partial(place_kernel, heads),
        out_shape=(bf16(state, width), bf16(count, width)),
        grid=(count // big,),
        in_specs=[smem(), whole(count, width), by_row(big, state), by_row(big, cols)],
        out_specs=(whole(state, width), by_row(big, width)),
        scratch_shapes=[f32(state, width), f32(count, width), f32(UNROLL, width)],
        compiler_params=params(),
        name="z_place",
    )(place, received, z_in_proj, z_cols)
    z_start = start_state(z_final, totals[:, 1], width)
    gated = pl.pallas_call(
        functools.partial(scan_gate_kernel, heads),
        out_shape=bf16(count, width),
        grid=(count // CHUNK,),
        in_specs=chunk_specs + [by_row(CHUNK, width)],
        out_specs=by_row(CHUNK, width),
        scratch_shapes=[f32(state, width)],
        compiler_params=params(),
        name="z_scan",
    )(u_z, z_in_proj, z_out_proj, z_cols, z_rows, z_start, gate_branch)

    mine = count // groups
    swapped = lax.all_to_all(gated.reshape(groups, mine, width), "head", 0, 0)
    model = out_weight.shape[1]
    tile = min(512, mine)
    return pl.pallas_call(
        tail_kernel,
        out_shape=bf16(mine, model),
        grid=(mine // tile,),
        in_specs=[
            pl.BlockSpec((groups, tile, width), lambda i: (0, i, 0)),
            whole(groups, width),
            whole(groups, width, model),
        ],
        out_specs=by_row(tile, model),
        compiler_params=params(),
        name="tail",
    )(swapped, gain, weight)


def solution(mesh):
    placed = (
        P("seq", "head"),
        P("seq", None),
        P("seq", None),
        P("head", "seq"),
        P("head", "seq"),
        P("seq"),
        P("seq", None),
        P("seq", None),
        P("head", "seq"),
        P("head", "seq"),
        P("seq", "head"),
        P("head"),
        P("head", None),
    )
    return jax.shard_map(
        body, mesh=mesh, in_specs=placed, out_specs=P(("seq", "head"), None), check_vma=False
    )
```

```python
import functools
import math

import jax
import jax.numpy as jnp
from jax import lax
from jax.experimental import pallas as pl
from jax.experimental.pallas import tpu as pltpu
from jax.sharding import PartitionSpec as P

CHUNK = 256
STEP = 1024
UNROLL = 32
VMEM = 56 * 1024 * 1024
LOG2E = math.log2(math.e)


def spread(columns, first, heads, width):
    head_width = width // heads
    rows = columns.shape[0]
    lanes = lax.broadcasted_iota(jnp.int32, (rows, width), 1)
    out = jnp.broadcast_to(columns[:, first : first + 1], (rows, width))
    for h in range(1, heads):
        column = jnp.broadcast_to(columns[:, first + h : first + h + 1], (rows, width))
        out = jnp.where(lanes >= h * head_width, column, out)
    return out


def add_state(total, u, b, columns, heads, first, mine):
    width = u.shape[1]
    scale = spread(columns, 3 * heads + first, mine, width)
    contrib = (u.astype(jnp.float32) * scale).astype(jnp.bfloat16)
    total[...] += lax.dot_general(
        b, contrib, (((0,), (0,)), ((), ())), preferred_element_type=jnp.float32
    )


def final_kernel(heads, first, mine, u_ref, b_ref, col_ref, out_ref, total):
    @pl.when(pl.program_id(0) == 0)
    def _():
        total[...] = jnp.zeros_like(total)

    add_state(total, u_ref[...], b_ref[...], col_ref[...], heads, first, mine)
    out_ref[...] = total[...].astype(out_ref.dtype)


def place_kernel(
    heads, first, mine, place_ref, recv_ref, b_ref, col_ref, out_ref, u_out, total, held, stage
):
    step = pl.program_id(0)

    @pl.when(step == 0)
    def _():
        total[...] = jnp.zeros_like(total)

        def rows(i, _):
            base = pl.multiple_of(i * UNROLL, UNROLL)
            stage[...] = recv_ref[pl.ds(base, UNROLL), :].astype(jnp.float32)
            for r in range(UNROLL):
                held[pl.ds(place_ref[base + r], 1), :] = stage[r : r + 1, :]
            return 0

        lax.fori_loop(0, recv_ref.shape[0] // UNROLL, rows, 0)

    count = b_ref.shape[0]
    u = held[pl.ds(pl.multiple_of(step * count, count), count), :].astype(jnp.bfloat16)
    u_out[...] = u
    add_state(total, u, b_ref[...], col_ref[...], heads, first, mine)
    out_ref[...] = total[...].astype(out_ref.dtype)


def chunk_result(heads, first, mine, u, b, c, columns, rows, state):
    count, width = u.shape
    head_width = width // mine
    scores = lax.dot_general(c, b, (((1,), (1,)), ((), ())), preferred_element_type=jnp.float32)
    lower = lax.broadcasted_iota(jnp.int32, (count, count), 0) >= lax.broadcasted_iota(
        jnp.int32, (count, count), 1
    )
    lanes = lax.broadcasted_iota(jnp.int32, (count, width), 1)
    grow = spread(columns, 2 * heads + first, mine, width)
    y = grow * jnp.dot(c, state[...].astype(jnp.bfloat16), preferred_element_type=jnp.float32)
    weights, inputs = [], []
    for h in range(mine):
        at = first + h
        factor = jnp.exp2(columns[:, at : at + 1] - rows[at : at + 1, :])
        weights.append(jnp.where(lower, scores * factor, 0.0).astype(jnp.bfloat16))
        own = (lanes >= h * head_width) & (lanes < (h + 1) * head_width)
        inputs.append(jnp.where(own, u, jnp.zeros_like(u)))
    y += jnp.dot(
        jnp.concatenate(weights, axis=1),
        jnp.concatenate(inputs, axis=0),
        preferred_element_type=jnp.float32,
    )
    scale = spread(columns, heads + first, mine, width)
    contrib = (u.astype(jnp.float32) * scale).astype(jnp.bfloat16)
    state[...] = grow[count - 1 : count, :] * state[...] + lax.dot_general(
        b, contrib, (((0,), (0,)), ((), ())), preferred_element_type=jnp.float32
    )
    return y


def scan_gather_kernel(
    heads,
    first,
    mine,
    pick_ref,
    u_ref,
    b_ref,
    c_ref,
    col_ref,
    row_ref,
    start_ref,
    out_ref,
    state,
    held,
    stage,
):
    step = pl.program_id(0)

    @pl.when(step == 0)
    def _():
        state[...] = start_ref[...]

    y = chunk_result(
        heads, first, mine, u_ref[...], b_ref[...], c_ref[...], col_ref[...], row_ref[0], state
    )
    held[pl.ds(pl.multiple_of(step * CHUNK, CHUNK), CHUNK), :] = y

    @pl.when(step == pl.num_programs(0) - 1)
    def _():
        def rows(i, _):
            base = pl.multiple_of(i * UNROLL, UNROLL)
            for r in range(UNROLL):
                stage[r : r + 1, :] = held[pl.ds(pick_ref[base + r], 1), :]
            out_ref[pl.ds(base, UNROLL), :] = stage[...].astype(out_ref.dtype)
            return 0

        lax.fori_loop(0, out_ref.shape[0] // UNROLL, rows, 0)


def scan_gate_kernel(
    heads, first, mine, u_ref, b_ref, c_ref, col_ref, row_ref, start_ref, gate_ref, out_ref, state
):
    @pl.when(pl.program_id(0) == 0)
    def _():
        state[...] = start_ref[...]

    y = chunk_result(
        heads, first, mine, u_ref[...], b_ref[...], c_ref[...], col_ref[...], row_ref[0], state
    )
    gate = gate_ref[...].astype(jnp.float32)
    out_ref[...] = (y * gate / (1.0 + jnp.exp(-gate))).astype(out_ref.dtype)


def tail_kernel(parts, *refs):
    w_ref, out_ref = refs[parts:]
    groups, rows, width = refs[0].shape
    square = jnp.zeros((rows, 1), jnp.float32)
    total = jnp.zeros(out_ref.shape, jnp.float32)
    for p in range(parts):
        for k in range(groups):
            sent = refs[p][k]
            g = sent.astype(jnp.float32)
            square += jnp.sum(g * g, axis=1, keepdims=True)
            total += jnp.dot(
                sent, w_ref[k, p * width : (p + 1) * width, :], preferred_element_type=jnp.float32
            )
    inverse = lax.rsqrt(square / (parts * groups * width) + 1e-05)
    out_ref[...] = (total * inverse).astype(out_ref.dtype)


def after(value, *others):
    return lax.optimization_barrier((value,) + others)[0]


def to_all(value, axis):
    count = lax.axis_size(axis)
    return lax.all_to_all(jnp.broadcast_to(value, (count,) + value.shape), axis, 0, 0)


def params():
    return pltpu.CompilerParams(vmem_limit_bytes=VMEM)


def cost(flops, moved):
    return pl.CostEstimate(flops=flops, bytes_accessed=moved, transcendentals=0)


def by_row(rows, width, at=0):
    return pl.BlockSpec((rows, width), lambda i: (i, at))


def whole(*shape):
    return pl.BlockSpec(shape, lambda i: (0,) * len(shape))


def smem():
    return pl.BlockSpec(memory_space=pltpu.SMEM)


def f32(*shape):
    return pltpu.VMEM(shape, jnp.float32)


def bf16(*shape):
    return jax.ShapeDtypeStruct(shape, jnp.bfloat16)


def decay_tables(log_decay, step):
    heads, count = log_decay.shape
    chunks = count // CHUNK
    ones = jnp.triu(jnp.ones((CHUNK, CHUNK), jnp.float32))
    g = log_decay.reshape(heads * chunks, CHUNK) * LOG2E
    cum = jnp.dot(g, ones, precision=lax.Precision.HIGHEST).reshape(heads, chunks, CHUNK)
    dt = step.reshape(heads, chunks, CHUNK)
    totals = cum[:, :, -1]
    after = lax.cumsum(totals, axis=1, reverse=True) - totals
    rest = totals[:, :, None] - cum
    columns = jnp.concatenate(
        [cum, jnp.exp2(rest) * dt, jnp.exp2(cum), jnp.exp2(rest + after[:, :, None]) * dt]
    )
    rows = (cum - jnp.log2(dt)).transpose(1, 0, 2)
    return columns.reshape(4 * heads, count).T, rows, jnp.sum(totals, axis=1)


def start_state(final, totals, width):
    me = lax.axis_index("seq")
    finals = to_all(final, "seq")
    count, heads = totals.shape
    place = jnp.arange(count)
    between = (place[None, :] > place[:, None]) & (place[None, :] < me)
    log = jnp.sum(jnp.where(between[:, :, None], totals[None], 0.0), axis=1)
    coef = jnp.where(place[:, None] < me, jnp.exp2(log), 0.0)
    coef = jnp.repeat(coef, width // heads, axis=1)
    return jnp.sum(coef[:, None, :] * finals.astype(jnp.float32), axis=0)


def body(
    x_inputs,
    x_in_proj,
    x_out_proj,
    x_log_decay,
    x_step,
    z_source,
    z_in_proj,
    z_out_proj,
    z_log_decay,
    z_step,
    gate_branch,
    norm_gain,
    out_weight,
):
    count, width = x_inputs.shape
    heads = x_log_decay.shape[0]
    state = x_in_proj.shape[1]
    peers = lax.axis_size("seq")
    groups = lax.axis_size("head")
    share = count // peers
    big = min(STEP, count)

    order, place = lax.sort((z_source, lax.iota(jnp.int32, count)), num_keys=1)
    pick = order.reshape(peers, share) - lax.iota(jnp.int32, peers)[:, None] * count
    pick = lax.all_to_all(pick, "seq", 0, 0).reshape(count)

    x_cols, x_rows, x_total = decay_tables(x_log_decay, x_step)
    z_cols, z_rows, z_total = decay_tables(z_log_decay, z_step)
    totals = to_all(jnp.stack([x_total, z_total]), "seq")
    scaled = (out_weight.astype(jnp.float32) * norm_gain[:, None]).astype(jnp.bfloat16)
    weight = to_all(scaled, "head")

    parts = 2 if width % 256 == 0 and heads % 2 == 0 else 1
    own = heads // parts
    part = width // parts
    cols = x_cols.shape[1]
    moved = 64 * count * part

    def chunk_specs(u_at):
        return [
            by_row(CHUNK, part, u_at),
            by_row(CHUNK, state),
            by_row(CHUNK, state),
            by_row(CHUNK, cols),
            pl.BlockSpec((1, heads, CHUNK), lambda i: (i, 0, 0)),
            pl.BlockSpec((state, part), lambda i: (0, u_at)),
        ]

    x_final = pl.pallas_call(
        functools.partial(final_kernel, heads, 0, heads),
        out_shape=bf16(state, width),
        grid=(count // big,),
        in_specs=[by_row(big, width), by_row(big, state), by_row(big, cols)],
        out_specs=whole(state, width),
        scratch_shapes=[f32(state, width)],
        compiler_params=params(),
        name="x_final",
    )(x_inputs, x_in_proj, x_cols)
    x_start = start_state(x_final, totals[:, 0], width)

    received, done = [], []
    for p in range(parts):
        sent = pl.pallas_call(
            functools.partial(scan_gather_kernel, heads, p * own, own),
            out_shape=bf16(count, part),
            grid=(count // CHUNK,),
            in_specs=[smem()] + chunk_specs(p),
            out_specs=whole(count, part),
            scratch_shapes=[f32(state, part), f32(count, part), f32(UNROLL, part)],
            compiler_params=params(),
            cost_estimate=cost(0, moved),
            name="x_scan_%d" % p,
        )(pick, x_inputs, x_in_proj, x_out_proj, x_cols, x_rows, after(x_start, *done))
        done.append(sent)
        received.append(lax.all_to_all(sent.reshape(peers, share, part), "seq", 0, 0))

    mine = count // groups
    swapped = []
    done.append(weight)
    for p in range(parts):
        arrived = after(received[p], *done).reshape(count, part)
        z_final, u_z = pl.pallas_call(
            functools.partial(place_kernel, heads, p * own, own),
            out_shape=(bf16(state, part), bf16(count, part)),
            grid=(count // big,),
            in_specs=[smem(), whole(count, part), by_row(big, state), by_row(big, cols)],
            out_specs=(whole(state, part), by_row(big, part)),
            scratch_shapes=[f32(state, part), f32(count, part), f32(UNROLL, part)],
            compiler_params=params(),
            cost_estimate=cost(0, moved // 2),
            name="z_place_%d" % p,
        )(place, arrived, z_in_proj, z_cols)
        z_start = start_state(z_final, totals[:, 1, p * own : (p + 1) * own], part)
        gated = pl.pallas_call(
            functools.partial(scan_gate_kernel, heads, p * own, own),
            out_shape=bf16(count, part),
            grid=(count // CHUNK,),
            in_specs=chunk_specs(0) + [by_row(CHUNK, part, p)],
            out_specs=by_row(CHUNK, part),
            scratch_shapes=[f32(state, part)],
            compiler_params=params(),
            cost_estimate=cost(0, moved),
            name="z_scan_%d" % p,
        )(u_z, z_in_proj, z_out_proj, z_cols, z_rows, z_start, gate_branch)
        done = [gated]
        swapped.append(lax.all_to_all(gated.reshape(groups, mine, part), "head", 0, 0))

    model = out_weight.shape[1]
    tile = min(512, mine)
    return pl.pallas_call(
        functools.partial(tail_kernel, parts),
        out_shape=bf16(mine, model),
        grid=(mine // tile,),
        in_specs=[pl.BlockSpec((groups, tile, part), lambda i: (0, i, 0))] * parts
        + [whole(groups, width, model)],
        out_specs=by_row(tile, model),
        compiler_params=params(),
        name="tail",
    )(*swapped, weight)


def solution(mesh):
    placed = (
        P("seq", "head"),
        P("seq", None),
        P("seq", None),
        P("head", "seq"),
        P("head", "seq"),
        P("seq"),
        P("seq", None),
        P("seq", None),
        P("head", "seq"),
        P("head", "seq"),
        P("seq", "head"),
        P("head"),
        P("head", None),
    )
    return jax.shard_map(
        body, mesh=mesh, in_specs=placed, out_specs=P(("seq", "head"), None), check_vma=False
    )
```

```python
import functools
import math

import jax
import jax.numpy as jnp
from jax import lax
from jax.experimental import pallas as pl
from jax.experimental.pallas import tpu as pltpu
from jax.sharding import PartitionSpec as P

CHUNK = 256
PAIR = 2
STEP = 1024
UNROLL = 32
VMEM = 56 * 1024 * 1024
LOG2E = math.log2(math.e)


def spread(columns, first, heads, width):
    head_width = width // heads
    rows = columns.shape[0]
    lanes = lax.broadcasted_iota(jnp.int32, (rows, width), 1)
    out = jnp.broadcast_to(columns[:, first : first + 1], (rows, width))
    for h in range(1, heads):
        column = jnp.broadcast_to(columns[:, first + h : first + h + 1], (rows, width))
        out = jnp.where(lanes >= h * head_width, column, out)
    return out


def add_state(total, u, b, columns, heads, first, mine):
    width = u.shape[1]
    scale = spread(columns, 3 * heads + first, mine, width)
    contrib = (u.astype(jnp.float32) * scale).astype(jnp.bfloat16)
    total[...] += lax.dot_general(
        b, contrib, (((0,), (0,)), ((), ())), preferred_element_type=jnp.float32
    )


def final_kernel(heads, first, mine, u_ref, b_ref, col_ref, out_ref, total):
    @pl.when(pl.program_id(0) == 0)
    def _():
        total[...] = jnp.zeros_like(total)

    add_state(total, u_ref[...], b_ref[...], col_ref[...], heads, first, mine)
    out_ref[...] = total[...].astype(out_ref.dtype)


def place_kernel(
    heads, first, mine, place_ref, recv_ref, b_ref, col_ref, out_ref, u_out, total, held, stage
):
    step = pl.program_id(0)

    @pl.when(step == 0)
    def _():
        total[...] = jnp.zeros_like(total)

        def rows(i, _):
            base = pl.multiple_of(i * UNROLL, UNROLL)
            stage[...] = recv_ref[pl.ds(base, UNROLL), :].astype(jnp.float32)
            for r in range(UNROLL):
                held[pl.ds(place_ref[base + r], 1), :] = stage[r : r + 1, :]
            return 0

        lax.fori_loop(0, recv_ref.shape[0] // UNROLL, rows, 0)

    count = b_ref.shape[0]
    u = held[pl.ds(pl.multiple_of(step * count, count), count), :].astype(jnp.bfloat16)
    u_out[...] = u
    add_state(total, u, b_ref[...], col_ref[...], heads, first, mine)
    out_ref[...] = total[...].astype(out_ref.dtype)


def chunk_result(heads, first, mine, u, b, c, columns, rows, state):
    count, width = u.shape
    head_width = width // mine
    scores = lax.dot_general(c, b, (((1,), (1,)), ((), ())), preferred_element_type=jnp.float32)
    lower = lax.broadcasted_iota(jnp.int32, (count, count), 0) >= lax.broadcasted_iota(
        jnp.int32, (count, count), 1
    )
    lanes = lax.broadcasted_iota(jnp.int32, (count, width), 1)
    grow = spread(columns, 2 * heads + first, mine, width)
    y = grow * jnp.dot(c, state[...].astype(jnp.bfloat16), preferred_element_type=jnp.float32)
    weights, inputs = [], []
    for h in range(mine):
        at = first + h
        factor = jnp.exp2(columns[:, at : at + 1] - rows[at : at + 1, :])
        weights.append(jnp.where(lower, scores * factor, 0.0).astype(jnp.bfloat16))
        own = (lanes >= h * head_width) & (lanes < (h + 1) * head_width)
        inputs.append(jnp.where(own, u, jnp.zeros_like(u)))
    y += jnp.dot(
        jnp.concatenate(weights, axis=1),
        jnp.concatenate(inputs, axis=0),
        preferred_element_type=jnp.float32,
    )
    scale = spread(columns, heads + first, mine, width)
    contrib = (u.astype(jnp.float32) * scale).astype(jnp.bfloat16)
    state[...] = grow[count - 1 : count, :] * state[...] + lax.dot_general(
        b, contrib, (((0,), (0,)), ((), ())), preferred_element_type=jnp.float32
    )
    return y


def pair_result(heads, first, mine, u_ref, b_ref, c_ref, col_ref, row_ref, state):
    results = []
    for j in range(PAIR):
        at = slice(j * CHUNK, (j + 1) * CHUNK)
        results.append(
            chunk_result(
                heads,
                first,
                mine,
                u_ref[at, :],
                b_ref[at, :],
                c_ref[at, :],
                col_ref[at, :],
                row_ref[j],
                state,
            )
        )
    return results


def scan_gather_kernel(
    heads,
    first,
    mine,
    pick_ref,
    u_ref,
    b_ref,
    c_ref,
    col_ref,
    row_ref,
    start_ref,
    out_ref,
    state,
    held,
    stage,
):
    step = pl.program_id(0)

    @pl.when(step == 0)
    def _():
        state[...] = start_ref[...]

    results = pair_result(heads, first, mine, u_ref, b_ref, c_ref, col_ref, row_ref, state)
    for j, y in enumerate(results):
        base = pl.multiple_of((step * PAIR + j) * CHUNK, CHUNK)
        held[pl.ds(base, CHUNK), :] = y

    @pl.when(step == pl.num_programs(0) - 1)
    def _():
        def rows(i, _):
            base = pl.multiple_of(i * UNROLL, UNROLL)
            for r in range(UNROLL):
                stage[r : r + 1, :] = held[pl.ds(pick_ref[base + r], 1), :]
            out_ref[pl.ds(base, UNROLL), :] = stage[...].astype(out_ref.dtype)
            return 0

        lax.fori_loop(0, out_ref.shape[0] // UNROLL, rows, 0)


def scan_gate_kernel(
    heads, first, mine, u_ref, b_ref, c_ref, col_ref, row_ref, start_ref, gate_ref, out_ref, state
):
    @pl.when(pl.program_id(0) == 0)
    def _():
        state[...] = start_ref[...]

    results = pair_result(heads, first, mine, u_ref, b_ref, c_ref, col_ref, row_ref, state)
    for j, y in enumerate(results):
        at = slice(j * CHUNK, (j + 1) * CHUNK)
        gate = gate_ref[at, :].astype(jnp.float32)
        out_ref[at, :] = (y * gate / (1.0 + jnp.exp(-gate))).astype(out_ref.dtype)


def tail_kernel(parts, *refs):
    w_ref, out_ref = refs[parts:]
    groups, rows, width = refs[0].shape
    square = jnp.zeros((rows, 1), jnp.float32)
    total = jnp.zeros(out_ref.shape, jnp.float32)
    for p in range(parts):
        for k in range(groups):
            sent = refs[p][k]
            g = sent.astype(jnp.float32)
            square += jnp.sum(g * g, axis=1, keepdims=True)
            total += jnp.dot(
                sent, w_ref[k, p * width : (p + 1) * width, :], preferred_element_type=jnp.float32
            )
    inverse = lax.rsqrt(square / (parts * groups * width) + 1e-05)
    out_ref[...] = (total * inverse).astype(out_ref.dtype)


def after(value, *others):
    return lax.optimization_barrier((value,) + others)[0]


def to_all(value, axis):
    count = lax.axis_size(axis)
    return lax.all_to_all(jnp.broadcast_to(value, (count,) + value.shape), axis, 0, 0)


def params():
    return pltpu.CompilerParams(vmem_limit_bytes=VMEM)


def cost(flops, moved):
    return pl.CostEstimate(flops=flops, bytes_accessed=moved, transcendentals=0)


def by_row(rows, width, at=0):
    return pl.BlockSpec((rows, width), lambda i: (i, at))


def whole(*shape):
    return pl.BlockSpec(shape, lambda i: (0,) * len(shape))


def smem():
    return pl.BlockSpec(memory_space=pltpu.SMEM)


def f32(*shape):
    return pltpu.VMEM(shape, jnp.float32)


def bf16(*shape):
    return jax.ShapeDtypeStruct(shape, jnp.bfloat16)


def decay_tables(log_decay, step):
    heads, count = log_decay.shape
    chunks = count // CHUNK
    ones = jnp.triu(jnp.ones((CHUNK, CHUNK), jnp.float32))
    g = log_decay.reshape(heads * chunks, CHUNK) * LOG2E
    cum = jnp.dot(g, ones, precision=lax.Precision.HIGHEST).reshape(heads, chunks, CHUNK)
    dt = step.reshape(heads, chunks, CHUNK)
    totals = cum[:, :, -1]
    after = lax.cumsum(totals, axis=1, reverse=True) - totals
    rest = totals[:, :, None] - cum
    columns = jnp.concatenate(
        [cum, jnp.exp2(rest) * dt, jnp.exp2(cum), jnp.exp2(rest + after[:, :, None]) * dt]
    )
    rows = (cum - jnp.log2(dt)).transpose(1, 0, 2)
    return columns.reshape(4 * heads, count).T, rows, jnp.sum(totals, axis=1)


def start_state(final, totals, width):
    me = lax.axis_index("seq")
    finals = to_all(final, "seq")
    count, heads = totals.shape
    place = jnp.arange(count)
    between = (place[None, :] > place[:, None]) & (place[None, :] < me)
    log = jnp.sum(jnp.where(between[:, :, None], totals[None], 0.0), axis=1)
    coef = jnp.where(place[:, None] < me, jnp.exp2(log), 0.0)
    coef = jnp.repeat(coef, width // heads, axis=1)
    return jnp.sum(coef[:, None, :] * finals.astype(jnp.float32), axis=0)


def body(
    x_inputs,
    x_in_proj,
    x_out_proj,
    x_log_decay,
    x_step,
    z_source,
    z_in_proj,
    z_out_proj,
    z_log_decay,
    z_step,
    gate_branch,
    norm_gain,
    out_weight,
):
    count, width = x_inputs.shape
    heads = x_log_decay.shape[0]
    state = x_in_proj.shape[1]
    peers = lax.axis_size("seq")
    groups = lax.axis_size("head")
    share = count // peers
    big = min(STEP, count)

    order, place = lax.sort((z_source, lax.iota(jnp.int32, count)), num_keys=1)
    pick = order.reshape(peers, share) - lax.iota(jnp.int32, peers)[:, None] * count
    pick = lax.all_to_all(pick, "seq", 0, 0).reshape(count)

    x_cols, x_rows, x_total = decay_tables(x_log_decay, x_step)
    z_cols, z_rows, z_total = decay_tables(z_log_decay, z_step)
    totals = to_all(jnp.stack([x_total, z_total]), "seq")
    scaled = (out_weight.astype(jnp.float32) * norm_gain[:, None]).astype(jnp.bfloat16)
    weight = to_all(scaled, "head")

    parts = 2 if width % 256 == 0 and heads % 2 == 0 else 1
    own = heads // parts
    part = width // parts
    cols = x_cols.shape[1]
    moved = 64 * count * part

    def chunk_specs(u_at, at):
        return [
            by_row(PAIR * CHUNK, part, u_at),
            by_row(PAIR * CHUNK, state),
            by_row(PAIR * CHUNK, state),
            by_row(PAIR * CHUNK, cols),
            pl.BlockSpec((PAIR, heads, CHUNK), lambda i: (i, 0, 0)),
            pl.BlockSpec((state, part), lambda i: (0, at)),
        ]

    x_final = pl.pallas_call(
        functools.partial(final_kernel, heads, 0, heads),
        out_shape=bf16(state, width),
        grid=(count // big,),
        in_specs=[by_row(big, width), by_row(big, state), by_row(big, cols)],
        out_specs=whole(state, width),
        scratch_shapes=[f32(state, width)],
        compiler_params=params(),
        name="x_final",
    )(x_inputs, x_in_proj, x_cols)
    x_start = start_state(x_final, totals[:, 0], width)

    received, done = [], []
    for p in range(parts):
        sent = pl.pallas_call(
            functools.partial(scan_gather_kernel, heads, p * own, own),
            out_shape=bf16(count, part),
            grid=(count // (PAIR * CHUNK),),
            in_specs=[smem()] + chunk_specs(p, p),
            out_specs=whole(count, part),
            scratch_shapes=[f32(state, part), f32(count, part), f32(UNROLL, part)],
            compiler_params=params(),
            cost_estimate=cost(0, moved),
            name="x_scan_%d" % p,
        )(pick, x_inputs, x_in_proj, x_out_proj, x_cols, x_rows, after(x_start, *done))
        done.append(sent)
        received.append(lax.all_to_all(sent.reshape(peers, share, part), "seq", 0, 0))

    mine = count // groups
    finals, inputs = [], []
    done.append(weight)
    for p in range(parts):
        arrived = after(received[p], *done).reshape(count, part)
        z_final, u_z = pl.pallas_call(
            functools.partial(place_kernel, heads, p * own, own),
            out_shape=(bf16(state, part), bf16(count, part)),
            grid=(count // big,),
            in_specs=[smem(), whole(count, part), by_row(big, state), by_row(big, cols)],
            out_specs=(whole(state, part), by_row(big, part)),
            scratch_shapes=[f32(state, part), f32(count, part), f32(UNROLL, part)],
            compiler_params=params(),
            cost_estimate=cost(0, moved // 2),
            name="z_place_%d" % p,
        )(place, arrived, z_in_proj, z_cols)
        finals.append(z_final)
        inputs.append(u_z)

    z_start = start_state(jnp.concatenate(finals, axis=1), totals[:, 1], width)
    swapped, done = [], []
    for p in range(parts):
        gated = pl.pallas_call(
            functools.partial(scan_gate_kernel, heads, p * own, own),
            out_shape=bf16(count, part),
            grid=(count // (PAIR * CHUNK),),
            in_specs=chunk_specs(0, p) + [by_row(PAIR * CHUNK, part, p)],
            out_specs=by_row(PAIR * CHUNK, part),
            scratch_shapes=[f32(state, part)],
            compiler_params=params(),
            cost_estimate=cost(0, moved),
            name="z_scan_%d" % p,
        )(inputs[p], z_in_proj, z_out_proj, z_cols, z_rows, after(z_start, *done), gate_branch)
        done = [gated]
        swapped.append(lax.all_to_all(gated.reshape(groups, mine, part), "head", 0, 0))

    model = out_weight.shape[1]
    tile = min(512, mine)
    return pl.pallas_call(
        functools.partial(tail_kernel, parts),
        out_shape=bf16(mine, model),
        grid=(mine // tile,),
        in_specs=[pl.BlockSpec((groups, tile, part), lambda i: (0, i, 0))] * parts
        + [whole(groups, width, model)],
        out_specs=by_row(tile, model),
        compiler_params=params(),
        name="tail",
    )(*swapped, weight)


def solution(mesh):
    placed = (
        P("seq", "head"),
        P("seq", None),
        P("seq", None),
        P("head", "seq"),
        P("head", "seq"),
        P("seq"),
        P("seq", None),
        P("seq", None),
        P("head", "seq"),
        P("head", "seq"),
        P("seq", "head"),
        P("head"),
        P("head", None),
    )
    return jax.shard_map(
        body, mesh=mesh, in_specs=placed, out_specs=P(("seq", "head"), None), check_vma=False
    )
```
